128 devices in a mesh: dp: 64 (over z, x, y_hi, core), rep: 2 (over y_lo).
Axes of the slice: x: 4, y: 4 (y_hi: 2, y_lo: 2; y = y_hi * 2 + y_lo), z: 4, core: 2. Of those that a mesh axis runs over, the one named last changes fastest.
Arguments:
- tokens: bfloat16 [200704, 1024], P(('dp', 'rep')), may hold values from -24 to 24
- cotangent: bfloat16 [200704, 2048], P(('dp', 'rep')), may hold values from -0.013671875 to 0.013671875
- global_tokens: bfloat16 [100352, 1024], P(('dp', 'rep')), may hold values from -6 to 6
- master: float32 [1024, 2048], P('dp'), may hold values from -0.1875 to 0.1875
- first_moment: float32 [1024, 2048], P('dp'), may hold values from -3 to 3
- second_moment: float32 [1024, 2048], P('dp'), may hold values from 0.05 to 2
- teacher: float32 [1024, 2048], P('dp'), may hold values from -0.1875 to 0.1875
Outputs:
- grad_input: bfloat16 [200704, 1024], P(('dp', 'rep'))
- teacher_hidden: bfloat16 [100352, 2048], P(('dp', 'rep'))
- new_master: float32 [1024, 2048], P('dp')
- new_first: float32 [1024, 2048], P('dp')
- new_second: float32 [1024, 2048], P('dp')
- new_teacher: float32 [1024, 2048], P('dp')
The draws below stay inside these ranges and needn't reach their ends.
All inputs are finite; a program needn't handle non-finite values.
Results may differ from the reference program's by a relative error of at most 0.0065.
Values may be sent and summed in bfloat16 or wider, within the bound.
No kernel may reach another device: no remote copies, remote signals or barrier semaphores. Data moves between devices by JAX's collectives and lax.ppermute only.
A program may use at most 128 MiB of HBM per device.

```python
import math
import jax
import jax.numpy as jnp
from jax import lax

D = 1024
FF = 2048
TOK_DEV = 1568
GTOK_DEV = 784
TOKENS = 200704
GTOKENS = 100352
N_DP = 64
N_REP = 2


def with_spikes(result, key, source, target, shards_of, factor):
    def block_of(position):
        return (jnp.arange(result.shape[position]) // (result.shape[position] // shards_of)).reshape((-1,) + (1,) * (result.ndim - 1 - position))

    near = jax.random.permutation(key, shards_of)[block_of(target)]
    far = (block_of(target) + shards_of // 2) % shards_of
    return jnp.where((block_of(source) == near) | (block_of(source) == far), factor * result, result)


def level_of(stream_key, shape, pieces, low, largest):
    def one(dim, blocks):
        steps = jax.random.uniform(jax.random.fold_in(jax.random.fold_in(stream_key, 6), dim), (blocks,), jnp.float32, low / len(pieces), largest / len(pieces))
        return jnp.repeat(jnp.exp(steps), shape[dim] // blocks).reshape((-1,) + (1,) * (len(shape) - dim - 1))

    loudness = one(*pieces[0])
    for cut in pieces[1:]:
        loudness = loudness * one(*cut)
    return loudness


def gaussian(own_key, shape, width, reach, shards=(), held_as=jnp.bfloat16):
    entries = width * jax.random.normal(own_key, shape, jnp.float32)
    if shards:
        entries = entries * level_of(own_key, shape, shards, -0.22, 0.18)
    return jnp.clip(entries, -reach, reach).astype(held_as)


def gaussian_with(rng, dims, deviation, limit, split, heavy, dtype=jnp.bfloat16):
    array = deviation * jax.random.normal(rng, dims, jnp.float32)
    if split:
        array = array * level_of(rng, dims, split, -0.22, 0.18)
    return jnp.clip(with_spikes(array, jax.random.fold_in(rng, 3), *heavy), -limit, limit).astype(dtype)


def setup_inputs(seed: int = 0) -> dict:
    streams_of = jax.random.split(jax.random.key(seed), 8)
    return {
        "tokens": gaussian_with(streams_of[0], (TOKENS, D), 1.0, 24.0, ((0, 128),), (0, 1, 128, 5.5)),
        "cotangent": gaussian(streams_of[1], (TOKENS, FF), ((TOK_DEV * N_DP * N_REP) ** -0.5), 0.013671875, ((0, 128),)),
        "global_tokens": gaussian(streams_of[2], (GTOKENS, D), 1.0, 6.0, ((0, 128),)),
        "master": gaussian(streams_of[3], (D, FF), D ** -0.5, 0.1875, ((0, 64),), jnp.float32),
        "first_moment": gaussian(streams_of[4], (D, FF), 0.5, 3.0, ((0, 64),), jnp.float32),
        "second_moment": jnp.clip(jnp.exp(math.log(2.0) - 3.6888794 * jax.random.uniform(streams_of[5], (D, FF), jnp.float32) ** level_of(streams_of[5], (D, FF), ((0, 64),), -0.2, 0.2)), 0.05, 2.0),
        "teacher": gaussian(streams_of[6], (D, FF), D ** -0.5, 0.1875, ((0, 64),), jnp.float32),
    }


beta_one = 0.9
beta_two = 0.999
learn_rate = 0.001
decay_rate = 0.04
ema_momentum = 0.996
adam_epsilon = 1e-08
norm_epsilon = 1e-06
bias_one = 0.9999734386011124
bias_two = 0.09520785288629038

def layer_norm(block_tokens):
    values = block_tokens.astype(jnp.float32)
    middle = lax.optimization_barrier(jnp.mean(values, axis=-1, keepdims=True))
    centred = values - middle
    inv_std = lax.rsqrt(lax.optimization_barrier(jnp.mean(centred * centred, axis=-1, keepdims=True)) + norm_epsilon)
    return (centred * inv_std, inv_std)

def gelu_parts(preact):
    cumul = 0.5 * (1.0 + lax.erf(preact * (1.0 / math.sqrt(2.0))))
    slope = cumul + preact * jnp.exp(-0.5 * preact * preact) * (1.0 / math.sqrt(2.0 * math.pi))
    return (preact * cumul, slope)

def reference(tokens, cotangent, global_tokens, master, first_moment, second_moment, teacher):
    student_weights = master.astype(jnp.bfloat16)

    def scan_step(gradient, block_pair):
        block_tokens, block_cot = block_pair
        centred, inv_std = layer_norm(block_tokens)
        normed = centred.astype(jnp.bfloat16)
        preact = jnp.dot(normed, student_weights, preferred_element_type=jnp.float32)
        unused, slope = gelu_parts(preact)
        delta = (block_cot.astype(jnp.float32) * slope).astype(jnp.bfloat16)
        back_normed = lax.dot_general(delta, student_weights, (((1,), (1,)), ((), ())), preferred_element_type=jnp.float32)
        mean_back = lax.optimization_barrier(jnp.mean(back_normed, axis=-1, keepdims=True))
        mean_cross = lax.optimization_barrier(jnp.mean(back_normed * centred, axis=-1, keepdims=True))
        grad_block = inv_std * (back_normed - mean_back - centred * mean_cross)
        gradient = gradient + lax.dot_general(normed, delta, (((0,), (0,)), ((), ())), preferred_element_type=jnp.float32)
        return (gradient, grad_block.astype(jnp.bfloat16))
    stacked_tokens = tokens.reshape((-1, TOK_DEV, D))
    stacked_cot = cotangent.reshape((-1, TOK_DEV, FF))
    gradient, grad_blocks = lax.scan(scan_step, jnp.zeros((D, FF), jnp.float32), (stacked_tokens, stacked_cot))
    grad_input = grad_blocks.reshape((-1, D))
    new_first = beta_one * first_moment + (1.0 - beta_one) * gradient
    new_second = beta_two * second_moment + (1.0 - beta_two) * gradient * gradient
    update = new_first / bias_one / (jnp.sqrt(new_second / bias_two) + adam_epsilon)
    new_master = master - learn_rate * (update + decay_rate * master)
    new_teacher = ema_momentum * teacher + (1.0 - ema_momentum) * new_master
    teacher_weights = teacher.astype(jnp.bfloat16)

    def teacher_block(block_tokens):
        centred, inv_std = layer_norm(block_tokens)
        teacher_pre = jnp.dot(centred.astype(jnp.bfloat16), teacher_weights, preferred_element_type=jnp.float32)
        activated, unused = gelu_parts(teacher_pre)
        return activated.astype(jnp.bfloat16)
    teacher_hidden = lax.map(teacher_block, global_tokens.reshape((-1, GTOK_DEV, D))).reshape((-1, FF))
    return (grad_input, teacher_hidden, new_master, new_first, new_second, new_teacher)
```

```python
import math

import jax
import jax.numpy as jnp
from jax import lax
from jax.sharding import Mesh
from jax.sharding import PartitionSpec as P

beta_one = 0.9
beta_two = 0.999
learn_rate = 0.001
decay_rate = 0.04
ema_momentum = 0.996
adam_epsilon = 1e-08
norm_epsilon = 1e-06
bias_one = 0.9999734386011124
bias_two = 0.09520785288629038

CHIPS = ("z", "x", "yh")
SWAP = [(0, 1), (1, 0)]
bf16, f32 = jnp.bfloat16, jnp.float32


def layer_norm(block_tokens):
    values = block_tokens.astype(f32)
    middle = jnp.mean(values, axis=-1, keepdims=True)
    centred = values - middle
    inv_std = lax.rsqrt(jnp.mean(centred * centred, axis=-1, keepdims=True) + norm_epsilon)
    return (centred * inv_std, inv_std)


def gelu_parts(preact):
    cumul = 0.5 * (1.0 + lax.erf(preact * (1.0 / math.sqrt(2.0))))
    slope = cumul + preact * jnp.exp(-0.5 * preact * preact) * (1.0 / math.sqrt(2.0 * math.pi))
    return (preact * cumul, slope)


def adamw_update(gradient, master_rows, first_rows, second_rows, teacher_rows):
    new_first = beta_one * first_rows + (1.0 - beta_one) * gradient
    new_second = beta_two * second_rows + (1.0 - beta_two) * gradient * gradient
    update = new_first / bias_one / (jnp.sqrt(new_second / bias_two) + adam_epsilon)
    new_master = master_rows - learn_rate * (update + decay_rate * master_rows)
    new_teacher = ema_momentum * teacher_rows + (1.0 - ema_momentum) * new_master
    return (new_master, new_first, new_second, new_teacher)


def swap(block):
    return lax.ppermute(block, "core", SWAP)


def in_core_order(mine, theirs, axis):
    first = lax.axis_index("core") == 0
    return jnp.where(
        first,
        jnp.concatenate([mine, theirs], axis=axis),
        jnp.concatenate([theirs, mine], axis=axis),
    )


def columns_of(array, core):
    half = array.shape[1] // 2
    return lax.dynamic_slice_in_dim(array, core * half, half, axis=1)


def per_device(tokens, cotangent, global_tokens, master, first_moment, second_moment, teacher):
    core = lax.axis_index("core")
    teacher_weights = lax.all_gather(
        teacher.astype(bf16), ("z", "x", "yh", "core"), axis=0, tiled=True
    )

    rounded = master.astype(bf16)
    theirs = swap(columns_of(rounded, 1 - core))
    block = in_core_order(columns_of(rounded, core), theirs, 0)
    copies = jnp.broadcast_to(block[None], (32,) + block.shape).reshape(-1, block.shape[1])
    weights_own = lax.all_to_all(copies, CHIPS, 0, 0, tiled=True)
    weights_other = swap(weights_own)

    centred, inv_std = layer_norm(tokens)
    normed = centred.astype(bf16)

    def delta_of(weights, which):
        preact = jnp.dot(normed, weights, preferred_element_type=f32)
        unused, slope = gelu_parts(preact)
        return (columns_of(cotangent, which).astype(f32) * slope).astype(bf16)

    def gradient_of(delta):
        return lax.dot_general(normed, delta, (((0,), (0,)), ((), ())), preferred_element_type=f32)

    delta_own = delta_of(weights_own, core)
    delta_other = delta_of(weights_other, 1 - core)
    sent = swap(gradient_of(delta_other).astype(bf16))
    partial = (gradient_of(delta_own) + sent.astype(f32)).astype(bf16)
    pieces = lax.all_to_all(partial, CHIPS, 0, 0, tiled=True)
    group = jnp.sum(pieces.reshape(32, 32, -1).astype(f32), axis=0)
    group = lax.optimization_barrier(group.astype(bf16))
    group = group.astype(f32) + lax.ppermute(group, "yl", SWAP).astype(f32)
    mine = lax.dynamic_slice_in_dim(group, core * 16, 16, axis=0)
    other = lax.dynamic_slice_in_dim(group, (1 - core) * 16, 16, axis=0)
    gradient = in_core_order(mine, swap(other), 1)
    new_master, new_first, new_second, new_teacher = adamw_update(
        gradient, master, first_moment, second_moment, teacher
    )

    back = lax.dot_general(
        delta_own, weights_own, (((1,), (1,)), ((), ())), preferred_element_type=f32
    ) + lax.dot_general(
        delta_other, weights_other, (((1,), (1,)), ((), ())), preferred_element_type=f32
    )
    mean_back = jnp.mean(back, axis=-1, keepdims=True)
    mean_cross = jnp.mean(back * centred, axis=-1, keepdims=True)
    grad_input = (inv_std * (back - mean_back - centred * mean_cross)).astype(bf16)

    teacher_centred, unused_std = layer_norm(global_tokens)
    teacher_pre = jnp.dot(
        teacher_centred.astype(bf16), teacher_weights, preferred_element_type=f32
    )
    activated, unused_slope = gelu_parts(teacher_pre)
    return (grad_input, activated.astype(bf16), new_master, new_first, new_second, new_teacher)


def solution(mesh):
    split = Mesh(mesh.devices.reshape(4, 4, 2, 2, 2), ("z", "x", "yh", "core", "yl"))
    tokens = P(("z", "x", "yh", "core", "yl"), None)
    rows = P(("z", "x", "yh", "core"), None)
    return jax.shard_map(
        per_device,
        mesh=split,
        in_specs=(tokens, tokens, tokens, rows, rows, rows, rows),
        out_specs=(tokens, tokens, rows, rows, rows, rows),
        check_vma=False,
    )
```

```python
import math

import jax
import jax.numpy as jnp
from jax import lax
from jax.experimental import pallas as pl
from jax.experimental.pallas import tpu as pltpu
from jax.sharding import Mesh
from jax.sharding import PartitionSpec as P

beta_one = 0.9
beta_two = 0.999
learn_rate = 0.001
decay_rate = 0.04
ema_momentum = 0.996
adam_epsilon = 1e-08
norm_epsilon = 1e-06
bias_one = 0.9999734386011124
bias_two = 0.09520785288629038

SWAP = [(0, 1), (1, 0)]
ACROSS = [(0, 3), (3, 0), (1, 2), (2, 1)]
EVEN = ("zh", "xh")
STEPS = ((1, 0), (0, 1), (-1, -1))
bf16, f32 = jnp.bfloat16, jnp.float32


def params():
    return pltpu.CompilerParams(vmem_limit_bytes=48 * 1024 * 1024)


def cost(flops, bytes_accessed):
    return pl.CostEstimate(flops=flops, bytes_accessed=bytes_accessed, transcendentals=0)


def layer_norm(block_tokens):
    values = block_tokens.astype(f32)
    middle = jnp.mean(values, axis=-1, keepdims=True)
    centred = values - middle
    inv_std = lax.rsqrt(jnp.mean(centred * centred, axis=-1, keepdims=True) + norm_epsilon)
    return (centred * inv_std, inv_std)


def gelu_parts(preact):
    cumul = 0.5 * (1.0 + lax.erf(preact * (1.0 / math.sqrt(2.0))))
    slope = cumul + preact * jnp.exp(-0.5 * preact * preact) * (1.0 / math.sqrt(2.0 * math.pi))
    return (preact * cumul, slope)


def adamw_update(gradient, master_rows, first_rows, second_rows, teacher_rows):
    new_first = beta_one * first_rows + (1.0 - beta_one) * gradient
    new_second = beta_two * second_rows + (1.0 - beta_two) * gradient * gradient
    update = new_first / bias_one / (jnp.sqrt(new_second / bias_two) + adam_epsilon)
    new_master = master_rows - learn_rate * (update + decay_rate * master_rows)
    new_teacher = ema_momentum * teacher_rows + (1.0 - ema_momentum) * new_master
    return (new_master, new_first, new_second, new_teacher)


def swap(block):
    return lax.ppermute(block, "core", SWAP)


def across(block):
    return lax.ppermute(block, ("yh", "yl"), ACROSS)


def shifted(block, step, sign):
    moves = [
        (4 * z + x, 4 * ((z + sign * step[0]) % 4) + (x + sign * step[1]) % 4)
        for z in range(4)
        for x in range(4)
    ]
    return lax.ppermute(block, ("zh", "zl", "xh", "xl"), moves)


def in_order(mine, theirs, axis_name, axis):
    first = lax.axis_index(axis_name) == 0
    return jnp.where(
        first,
        jnp.concatenate([mine, theirs], axis=axis),
        jnp.concatenate([theirs, mine], axis=axis),
    )


def columns_of(array, core):
    half = array.shape[-1] // 2
    return lax.dynamic_slice_in_dim(array, core * half, half, axis=array.ndim - 1)


def even_gather(block):
    copies = jnp.broadcast_to(block[None], (4,) + block.shape)
    return lax.all_to_all(copies, EVEN, 0, 0, tiled=True)


def class_of(step):
    return (
        (lax.axis_index("zl") + step[0]) % 2,
        (lax.axis_index("xl") + step[1]) % 2,
    )


def assemble_kernel(class_ref, *refs):
    whole_ref = refs[4]
    for part_ref, (dz, dx) in zip(refs[:4], ((0, 0),) + STEPS):
        zl = lax.rem(class_ref[0] + dz % 2, 2)
        xl = lax.rem(class_ref[1] + dx % 2, 2)
        for even in range(4):
            chip = (4 * (even // 2) + 2 * zl + even % 2) * 2 + xl
            whole_ref[pl.ds(pl.multiple_of(64 * chip, 64), 64), :] = part_ref[even]


def assemble(parts):
    parity = jnp.stack([lax.axis_index("zl"), lax.axis_index("xl")]).astype(jnp.int32)
    half = parts[0].shape[-1]
    tile = half // 2
    piece = pl.BlockSpec((4, 64, tile), lambda i, parity: (0, 0, i))
    return pl.pallas_call(
        assemble_kernel,
        grid_spec=pltpu.PrefetchScalarGridSpec(
            num_scalar_prefetch=1,
            grid=(2,),
            in_specs=[piece] * 4,
            out_specs=pl.BlockSpec((1024, tile), lambda i, parity: (0, i)),
        ),
        out_shape=jax.ShapeDtypeStruct((1024, half), parts[0].dtype),
        compiler_params=params(),
        cost_estimate=cost(0, 4 * 1024 * half),
    )(parity, *parts)


def steps_of(part):
    return [part] + [shifted(part, step, 1) for step in STEPS]


def norm_kernel(tokens_ref, normed_ref):
    normed_ref[...] = layer_norm(tokens_ref[...])[0].astype(bf16)


def norm_call(tokens):
    rows, width = tokens.shape
    spec = pl.BlockSpec((784, width), lambda i: (i, 0))
    return pl.pallas_call(
        norm_kernel,
        grid=(rows // 784,),
        in_specs=[spec],
        out_specs=spec,
        out_shape=jax.ShapeDtypeStruct((rows, width), bf16),
        compiler_params=params(),
        cost_estimate=cost(0, 1024),
    )(tokens)


def input_kernel(delta_own_ref, delta_other_ref, own_ref, other_ref, tokens_ref, out_ref):
    dims = (((1,), (1,)), ((), ()))
    back = lax.dot_general(delta_own_ref[...], own_ref[...], dims, preferred_element_type=f32)
    back += lax.dot_general(delta_other_ref[...], other_ref[...], dims, preferred_element_type=f32)
    centred, inv_std = layer_norm(tokens_ref[...])
    mean_back = jnp.mean(back, axis=-1, keepdims=True)
    mean_cross = jnp.mean(back * centred, axis=-1, keepdims=True)
    out_ref[...] = (inv_std * (back - mean_back - centred * mean_cross)).astype(bf16)


def input_call(delta_own, delta_other, own, other, tokens):
    rows, width = tokens.shape
    half = own.shape[1]
    deltas = pl.BlockSpec((784, half), lambda i: (i, 0))
    weights = pl.BlockSpec((width, half), lambda i: (0, 0))
    spec = pl.BlockSpec((784, width), lambda i: (i, 0))
    return pl.pallas_call(
        input_kernel,
        grid=(rows // 784,),
        in_specs=[deltas, deltas, weights, weights, spec],
        out_specs=spec,
        out_shape=jax.ShapeDtypeStruct((rows, width), bf16),
        compiler_params=params(),
        cost_estimate=cost(4 * rows * width * half, 0),
    )(delta_own, delta_other, own, other, tokens)


def hidden_kernel(core_ref, normed_ref, own_ref, other_ref, hidden_ref):
    normed = normed_ref[...]
    half, step = own_ref.shape[1], 256
    for which, weights_ref in ((0, own_ref), (1, other_ref)):
        start = jnp.where(core_ref[0] == which, 0, half)
        for n in range(0, half, step):
            pre = jnp.dot(normed, weights_ref[:, n : n + step], preferred_element_type=f32)
            columns = pl.ds(pl.multiple_of(start + n, step), step)
            hidden_ref[:, columns] = gelu_parts(pre)[0].astype(bf16)


def hidden_call(normed, own, other, core):
    rows, width = normed.shape
    half, tile = own.shape[1], rows // 2
    weights = pl.BlockSpec((width, half), lambda i, core: (0, 0))
    return pl.pallas_call(
        hidden_kernel,
        grid_spec=pltpu.PrefetchScalarGridSpec(
            num_scalar_prefetch=1,
            grid=(rows // tile,),
            in_specs=[pl.BlockSpec((tile, width), lambda i, core: (i, 0)), weights, weights],
            out_specs=pl.BlockSpec((tile, 2 * half), lambda i, core: (i, 0)),
        ),
        out_shape=jax.ShapeDtypeStruct((rows, 2 * half), bf16),
        compiler_params=params(),
        cost_estimate=cost(4 * rows * width * half, 0),
    )(core.astype(jnp.int32).reshape(1), normed, own, other)


def step_reduce(kept, got):
    kept = kept.reshape(2, 2, 2, 2, 64, -1)
    got = got.reshape(kept.shape)
    total = None
    for step in ((0, 0),) + STEPS:
        zl, xl = class_of(step)
        start, size = (0, zl, 0, xl, 0, 0), (2, 1, 2, 1) + kept.shape[4:]
        piece = lax.dynamic_slice(kept, start, size) + lax.dynamic_slice(got, start, size).astype(f32)
        if step == (0, 0):
            total = piece
        else:
            total = total + shifted(piece.astype(bf16), step, -1).astype(f32)
    return total.astype(bf16).reshape((4,) + kept.shape[4:])


def per_device(tokens, cotangent, global_tokens, master, first_moment, second_moment, teacher):
    core = lax.axis_index("core")
    yh = lax.axis_index("yh")

    rounded = jnp.stack([master.astype(bf16), teacher.astype(bf16)])
    pair = in_order(columns_of(rounded, core), swap(columns_of(rounded, 1 - core)), "core", 1)
    blocks = in_order(pair, across(pair), "yh", 1)
    blocks, tokens, global_tokens = lax.optimization_barrier((blocks, tokens, global_tokens))
    both_parts = even_gather(blocks)
    normed, teacher_normed, both_parts = lax.optimization_barrier(
        (norm_call(tokens), norm_call(global_tokens), both_parts)
    )
    weights_own = assemble(steps_of(both_parts[:, 0]))
    normed, weights_own, teacher_part = lax.optimization_barrier(
        (normed, weights_own, both_parts[:, 1])
    )
    weights_other = swap(weights_own)

    def delta_of(weights, which):
        preact = jnp.dot(normed, weights, preferred_element_type=f32)
        unused, slope = gelu_parts(preact)
        return (columns_of(cotangent, which).astype(f32) * slope).astype(bf16)

    def gradient_of(delta):
        return lax.dot_general(normed, delta, (((0,), (0,)), ((), ())), preferred_element_type=f32)

    delta_own = delta_of(weights_own, core)
    teacher_parts = steps_of(teacher_part)
    delta_own, weights_other = lax.optimization_barrier((delta_own, weights_other))
    delta_other = delta_of(weights_other, 1 - core)
    given, teacher_parts = lax.optimization_barrier(
        (gradient_of(delta_other).astype(bf16), teacher_parts)
    )
    kept, delta_own, delta_other = lax.optimization_barrier(
        (gradient_of(delta_own), delta_own, delta_other)
    )
    class_sum = step_reduce(kept, swap(given))
    grad_input = input_call(delta_own, delta_other, weights_own, weights_other, tokens)

    class_sum, grad_input, teacher_parts = lax.optimization_barrier(
        (class_sum, grad_input, teacher_parts)
    )
    pieces = lax.all_to_all(class_sum, EVEN, 0, 0, tiled=True)
    teacher_own = assemble(teacher_parts)
    teacher_hidden = hidden_call(teacher_normed, teacher_own, swap(teacher_own), core)

    pieces, teacher_hidden = lax.optimization_barrier((pieces, teacher_hidden))

    plane = jnp.sum(pieces.astype(f32), axis=0)
    mine = lax.dynamic_slice_in_dim(plane, yh * 32, 32, axis=0)
    other = lax.dynamic_slice_in_dim(plane, (1 - yh) * 32, 32, axis=0)
    group = mine + across(other.astype(bf16)).astype(f32)
    group = lax.optimization_barrier(group.astype(bf16))
    group = group.astype(f32) + lax.ppermute(group, "yl", SWAP).astype(f32)
    mine = lax.dynamic_slice_in_dim(group, core * 16, 16, axis=0)
    other = lax.dynamic_slice_in_dim(group, (1 - core) * 16, 16, axis=0)
    gradient = in_order(mine, swap(other), "core", 1)
    new_master, new_first, new_second, new_teacher = adamw_update(
        gradient, master, first_moment, second_moment, teacher
    )
    return (grad_input, teacher_hidden, new_master, new_first, new_second, new_teacher)


def solution(mesh):
    names = ("zh", "zl", "xh", "xl", "yh", "core", "yl")
    split = Mesh(mesh.devices.reshape((2,) * 7), names)
    tokens = P(names, None)
    rows = P(names[:-1], None)
    return jax.shard_map(
        per_device,
        mesh=split,
        in_specs=(tokens, tokens, tokens, rows, rows, rows, rows),
        out_specs=(tokens, tokens, rows, rows, rows, rows),
        check_vma=False,
    )
```

```python
import math

import jax
import jax.numpy as jnp
from jax import lax
from jax.experimental import pallas as pl
from jax.experimental.pallas import tpu as pltpu
from jax.sharding import Mesh
from jax.sharding import PartitionSpec as P

beta_one = 0.9
beta_two = 0.999
learn_rate = 0.001
decay_rate = 0.04
ema_momentum = 0.996
adam_epsilon = 1e-08
norm_epsilon = 1e-06
bias_one = 0.9999734386011124
bias_two = 0.09520785288629038

SWAP = [(0, 1), (1, 0)]
CHIPS = ("z", "x", "yh")
bf16, f32 = jnp.bfloat16, jnp.float32


def params(mebibytes):
    return pltpu.CompilerParams(vmem_limit_bytes=mebibytes * 1024 * 1024)


def cost(flops, bytes_accessed):
    return pl.CostEstimate(flops=flops, bytes_accessed=bytes_accessed, transcendentals=0)


def layer_norm(block_tokens):
    values = block_tokens.astype(f32)
    middle = jnp.mean(values, axis=-1, keepdims=True)
    centred = values - middle
    inv_std = lax.rsqrt(jnp.mean(centred * centred, axis=-1, keepdims=True) + norm_epsilon)
    return (centred * inv_std, inv_std)


def gelu_parts(preact):
    cumul = 0.5 * (1.0 + lax.erf(preact * (1.0 / math.sqrt(2.0))))
    slope = cumul + preact * jnp.exp(-0.5 * preact * preact) * (1.0 / math.sqrt(2.0 * math.pi))
    return (preact * cumul, slope)


def adamw_update(gradient, master_rows, first_rows, second_rows, teacher_rows):
    new_first = beta_one * first_rows + (1.0 - beta_one) * gradient
    new_second = beta_two * second_rows + (1.0 - beta_two) * gradient * gradient
    update = new_first / bias_one / (jnp.sqrt(new_second / bias_two) + adam_epsilon)
    new_master = master_rows - learn_rate * (update + decay_rate * master_rows)
    new_teacher = ema_momentum * teacher_rows + (1.0 - ema_momentum) * new_master
    return (new_master, new_first, new_second, new_teacher)


def swap(block):
    return lax.ppermute(block, "core", SWAP)


def in_order(mine, theirs, axis_name, axis):
    first = lax.axis_index(axis_name) == 0
    return jnp.where(
        first,
        jnp.concatenate([mine, theirs], axis=axis),
        jnp.concatenate([theirs, mine], axis=axis),
    )


def columns_of(array, core):
    half = array.shape[-1] // 2
    return lax.dynamic_slice_in_dim(array, core * half, half, axis=array.ndim - 1)


def half_block(rows, core):
    return in_order(columns_of(rows, core), swap(columns_of(rows, 1 - core)), "core", 0)


def copies_of(block):
    return jnp.broadcast_to(block[None], (32,) + block.shape)


def exchanged(blocks):
    return lax.all_to_all(blocks, CHIPS, 0, 0, tiled=True)


def norm_kernel(tokens_ref, block_ref, normed_ref, copies_ref):
    normed_ref[...] = layer_norm(tokens_ref[...])[0].astype(bf16)
    copies_ref[...] = jnp.broadcast_to(block_ref[...][None], copies_ref.shape)


def norm_call(tokens, block, steps):
    rows, width = tokens.shape
    spec = pl.BlockSpec((rows // steps, width), lambda i: (i, 0))
    return pl.pallas_call(
        norm_kernel,
        grid=(steps,),
        in_specs=[spec, pl.BlockSpec(block.shape, lambda i: (0, 0))],
        out_specs=[spec, pl.BlockSpec((32 // steps,) + block.shape, lambda i: (i, 0, 0))],
        out_shape=[
            jax.ShapeDtypeStruct((rows, width), bf16),
            jax.ShapeDtypeStruct((32,) + block.shape, block.dtype),
        ],
        compiler_params=params(LIMIT),
        cost_estimate=cost(0, 1024),
    )(tokens, block)


def teacher_norm_kernel(tokens_ref, normed_ref):
    normed_ref[...] = layer_norm(tokens_ref[...])[0].astype(bf16)


def teacher_norm_call(tokens):
    spec = pl.BlockSpec(tokens.shape, lambda i: (0, 0))
    return pl.pallas_call(
        teacher_norm_kernel,
        grid=(1,),
        in_specs=[spec],
        out_specs=spec,
        out_shape=jax.ShapeDtypeStruct(tokens.shape, bf16),
        compiler_params=params(LIMIT),
        cost_estimate=cost(0, 1024),
    )(tokens)


LIMIT = 60
TILES = ((0, 512), (512, 512), (1024, 544))
PIECES = 4


def start_all(copies):
    for copy in copies:
        copy.start()
    return copies


def wait_all(copies):
    for copy in copies:
        copy.wait()


def store_delta(which_ref, hbm, vmem, sems):
    normed_hbm, weights_hbm, cotangent_hbm, delta_hbm = hbm
    normed_ref, weights_ref, cotangent_ref, delta_ref = vmem
    half = weights_ref.shape[1]
    columns = pl.ds(pl.multiple_of(which_ref[0] * half, half), half)
    weights_in = start_all([pltpu.make_async_copy(weights_hbm, weights_ref, sems.at[0])])
    tiles_in = []
    for n, (first, size) in enumerate(TILES):
        rows = pl.ds(first, size)
        tiles_in.append(
            start_all(
                [
                    pltpu.make_async_copy(
                        normed_hbm.at[rows], normed_ref.at[rows], sems.at[1 + 2 * n]
                    ),
                    pltpu.make_async_copy(
                        cotangent_hbm.at[rows, columns], cotangent_ref.at[rows], sems.at[2 + 2 * n]
                    ),
                ]
            )
        )
    out = []
    wait_all(weights_in)
    for n, (first, size) in enumerate(TILES):
        rows = pl.ds(first, size)
        wait_all(tiles_in[n])
        for m in range(0, half, 256):
            part = pl.ds(m, 256)
            preact = jnp.dot(normed_ref[rows, :], weights_ref[:, part], preferred_element_type=f32)
            slope = gelu_parts(preact)[1]
            delta_ref[rows, part] = (cotangent_ref[rows, part].astype(f32) * slope).astype(bf16)
        copy = pltpu.make_async_copy(delta_ref.at[rows], delta_hbm.at[rows], sems.at[7 + n])
        out += start_all([copy])
    return out


def gradient_piece(normed_ref, delta_ref, n, step):
    return lax.dot_general(
        normed_ref[:, n * step : (n + 1) * step],
        delta_ref[...],
        (((0,), (0,)), ((), ())),
        preferred_element_type=f32,
    )


def own_kernel(which_ref, normed_hbm, weights_hbm, cotangent_hbm, delta_hbm, *refs):
    sums_hbm, vmem, (sums_ref, sems) = refs[:PIECES], refs[PIECES:-2], refs[-2:]
    hbm = (normed_hbm, weights_hbm, cotangent_hbm, delta_hbm)
    out = store_delta(which_ref, hbm, vmem, sems)
    step = sums_ref.shape[0] // PIECES
    for n in range(PIECES):
        rows = pl.ds(n * step, step)
        sums_ref[rows, :] = gradient_piece(vmem[0], vmem[3], n, step).astype(bf16)
        copy = pltpu.make_async_copy(sums_ref.at[rows], sums_hbm[n], sems.at[10 + n])
        out += start_all([copy])
    wait_all(out)


def other_kernel(which_ref, normed_hbm, weights_hbm, cotangent_hbm, delta_hbm, *refs):
    hbm = (normed_hbm, weights_hbm, cotangent_hbm, delta_hbm)
    wait_all(store_delta(which_ref, hbm, refs[:-1], refs[-1]))


def sum_kernel(normed_hbm, delta_hbm, *refs):
    got_hbm, (sums_hbm, normed_ref, delta_ref, got_ref, sums_ref, sems) = refs[:PIECES], refs[PIECES:]
    step = sums_ref.shape[0] // PIECES
    delta_in = start_all([pltpu.make_async_copy(delta_hbm, delta_ref, sems.at[0])])
    pieces_in = []
    for n in range(PIECES):
        columns, rows = pl.ds(n * step, step), pl.ds(n * step, step)
        pieces_in.append(
            start_all(
                [
                    pltpu.make_async_copy(
                        normed_hbm.at[:, columns], normed_ref.at[:, columns], sems.at[1 + 2 * n]
                    ),
                    pltpu.make_async_copy(got_hbm[n], got_ref.at[rows], sems.at[2 + 2 * n]),
                ]
            )
        )
    out = []
    wait_all(delta_in)
    for n in range(PIECES):
        rows = pl.ds(n * step, step)
        wait_all(pieces_in[n])
        total = gradient_piece(normed_ref, delta_ref, n, step) + got_ref[rows, :].astype(f32)
        sums_ref[rows, :] = total.astype(bf16)
        copy = pltpu.make_async_copy(
            sums_ref.at[rows], sums_hbm.at[rows], sems.at[1 + 2 * PIECES + n]
        )
        out += start_all([copy])
    wait_all(out)


def local_call(kernel, outs, scratch, semaphores, *arrays):
    anywhere = pl.BlockSpec(memory_space=pl.ANY)
    return pl.pallas_call(
        kernel,
        in_specs=[
            pl.BlockSpec(memory_space=pltpu.SMEM) if array.ndim == 1 else anywhere
            for array in arrays
        ],
        out_specs=[anywhere] * len(outs),
        out_shape=[jax.ShapeDtypeStruct(shape, bf16) for shape in outs],
        scratch_shapes=[pltpu.VMEM(shape, bf16) for shape in scratch]
        + [pltpu.SemaphoreType.DMA((semaphores,))],
        compiler_params=params(LIMIT),
        cost_estimate=cost(0, 1024),
    )(*arrays)


def input_kernel(delta_own_ref, delta_other_ref, own_ref, other_ref, tokens_ref, out_ref):
    dims = (((1,), (1,)), ((), ()))
    back = lax.dot_general(delta_own_ref[...], own_ref[...], dims, preferred_element_type=f32)
    back += lax.dot_general(delta_other_ref[...], other_ref[...], dims, preferred_element_type=f32)
    centred, inv_std = layer_norm(tokens_ref[...])
    mean_back = jnp.mean(back, axis=-1, keepdims=True)
    mean_cross = jnp.mean(back * centred, axis=-1, keepdims=True)
    out_ref[...] = (inv_std * (back - mean_back - centred * mean_cross)).astype(bf16)


def input_call(delta_own, delta_other, own, other, tokens):
    rows, width = tokens.shape
    half = own.shape[1]
    deltas = pl.BlockSpec((784, half), lambda i: (i, 0))
    weights = pl.BlockSpec((width, half), lambda i: (0, 0))
    spec = pl.BlockSpec((784, width), lambda i: (i, 0))
    return pl.pallas_call(
        input_kernel,
        grid=(rows // 784,),
        in_specs=[deltas, deltas, weights, weights, spec],
        out_specs=spec,
        out_shape=jax.ShapeDtypeStruct((rows, width), bf16),
        compiler_params=params(LIMIT),
        cost_estimate=cost(4 * rows * width * half, 0),
    )(delta_own, delta_other, own, other, tokens)


def hidden_kernel(core_ref, normed_ref, own_ref, other_ref, hidden_ref):
    normed = normed_ref[...]
    half, step = own_ref.shape[1], 256
    for which, weights_ref in ((0, own_ref), (1, other_ref)):
        start = jnp.where(core_ref[0] == which, 0, half)
        for n in range(0, half, step):
            pre = jnp.dot(normed, weights_ref[:, n : n + step], preferred_element_type=f32)
            columns = pl.ds(pl.multiple_of(start + n, step), step)
            hidden_ref[:, columns] = gelu_parts(pre)[0].astype(bf16)


def hidden_call(normed, own, other, core):
    rows, width = normed.shape
    half, tile = own.shape[1], rows // 2
    weights = pl.BlockSpec((width, half), lambda i, core: (0, 0))
    return pl.pallas_call(
        hidden_kernel,
        grid_spec=pltpu.PrefetchScalarGridSpec(
            num_scalar_prefetch=1,
            grid=(rows // tile,),
            in_specs=[pl.BlockSpec((tile, width), lambda i, core: (i, 0)), weights, weights],
            out_specs=pl.BlockSpec((tile, 2 * half), lambda i, core: (i, 0)),
        ),
        out_shape=jax.ShapeDtypeStruct((rows, 2 * half), bf16),
        compiler_params=params(LIMIT),
        cost_estimate=cost(4 * rows * width * half, 0),
    )(core.astype(jnp.int32).reshape(1), normed, own, other)


def per_device(tokens, cotangent, global_tokens, master, first_moment, second_moment, teacher):
    core = lax.axis_index("core")

    width, half = tokens.shape[1], cotangent.shape[1] // 2

    copies = copies_of(half_block(master.astype(bf16), core))
    copies, tokens, global_tokens, teacher_rows = lax.optimization_barrier(
        (copies, tokens, global_tokens, teacher)
    )
    weights_own = exchanged(copies).reshape(width, half)
    teacher_block = half_block(teacher_rows.astype(bf16), core)
    normed, teacher_copies = norm_call(tokens, teacher_block, 2)
    teacher_normed = teacher_norm_call(global_tokens)
    normed, teacher_normed, teacher_copies, weights_own = lax.optimization_barrier(
        (normed, teacher_normed, teacher_copies, weights_own)
    )
    teacher_own = exchanged(teacher_copies).reshape(width, half)
    weights_other = swap(weights_own)

    rows = tokens.shape[0]
    delta, square = (rows, half), (width, half)
    vmem = [(rows, width), square, delta, delta]
    which = core.astype(jnp.int32).reshape(1)
    delta_own, *given = local_call(
        own_kernel,
        [delta] + [(width // PIECES, half)] * PIECES,
        vmem + [square],
        10 + PIECES,
        which,
        normed,
        weights_own,
        cotangent,
    )
    got = [swap(piece) for piece in given]
    (delta_other,) = local_call(
        other_kernel, [delta], vmem, 10, 1 - which, normed, weights_other, cotangent
    )
    (partial,) = local_call(
        sum_kernel,
        [square],
        [(rows, width), delta, square, square],
        1 + 3 * PIECES,
        normed,
        delta_other,
        *got,
    )
    pieces = exchanged(partial.reshape(32, 32, half))
    partial, delta_own, delta_other, teacher_own = lax.optimization_barrier(
        (partial, delta_own, delta_other, teacher_own)
    )
    grad_input = input_call(delta_own, delta_other, weights_own, weights_other, tokens)
    teacher_hidden = hidden_call(teacher_normed, teacher_own, swap(teacher_own), core)
    pieces, teacher_hidden, grad_input = lax.optimization_barrier(
        (pieces, teacher_hidden, grad_input)
    )
    group = jnp.sum(pieces.astype(f32), axis=0)
    group = lax.optimization_barrier(group.astype(bf16))
    mine = lax.dynamic_slice_in_dim(group, core * 16, 16, axis=0)
    other = lax.dynamic_slice_in_dim(group, (1 - core) * 16, 16, axis=0)
    here = mine.astype(f32) + lax.ppermute(mine, "yl", SWAP).astype(f32)
    diagonal = lax.ppermute(other, ("core", "yl"), [(0, 3), (1, 2), (2, 1), (3, 0)])
    there = swap(other).astype(f32) + diagonal.astype(f32)
    gradient = in_order(there, here, "core", 1)
    new_master, new_first, new_second, new_teacher = adamw_update(
        gradient, master, first_moment, second_moment, teacher
    )
    return (grad_input, teacher_hidden, new_master, new_first, new_second, new_teacher)


def solution(mesh):
    names = ("z", "x", "yh", "core", "yl")
    split = Mesh(mesh.devices.reshape(4, 4, 2, 2, 2), names)
    tokens = P(names, None)
    rows = P(names[:-1], None)
    return jax.shard_map(
        per_device,
        mesh=split,
        in_specs=(tokens, tokens, tokens, rows, rows, rows, rows),
        out_specs=(tokens, tokens, rows, rows, rows, rows),
        check_vma=False,
    )
```

```python
import math

import jax
import jax.numpy as jnp
from jax import lax
from jax.experimental import pallas as pl
from jax.experimental.pallas import tpu as pltpu
from jax.sharding import Mesh
from jax.sharding import PartitionSpec as P

beta_one = 0.9
beta_two = 0.999
learn_rate = 0.001
decay_rate = 0.04
ema_momentum = 0.996
adam_epsilon = 1e-08
norm_epsilon = 1e-06
bias_one = 0.9999734386011124
bias_two = 0.09520785288629038

SWAP = [(0, 1), (1, 0)]
ACROSS = [(0, 3), (3, 0), (1, 2), (2, 1)]
CHIPS = ("z", "x", "yh")
bf16, f32 = jnp.bfloat16, jnp.float32


def params(mebibytes):
    return pltpu.CompilerParams(vmem_limit_bytes=mebibytes * 1024 * 1024)


def cost(flops, bytes_accessed):
    return pl.CostEstimate(flops=flops, bytes_accessed=bytes_accessed, transcendentals=0)


def layer_norm(block_tokens):
    values = block_tokens.astype(f32)
    middle = jnp.mean(values, axis=-1, keepdims=True)
    centred = values - middle
    inv_std = lax.rsqrt(jnp.mean(centred * centred, axis=-1, keepdims=True) + norm_epsilon)
    return (centred * inv_std, inv_std)


def gelu_parts(preact):
    cumul = 0.5 * (1.0 + lax.erf(preact * (1.0 / math.sqrt(2.0))))
    slope = cumul + preact * jnp.exp(-0.5 * preact * preact) * (1.0 / math.sqrt(2.0 * math.pi))
    return (preact * cumul, slope)


def adamw_update(gradient, master_rows, first_rows, second_rows, teacher_rows):
    new_first = beta_one * first_rows + (1.0 - beta_one) * gradient
    new_second = beta_two * second_rows + (1.0 - beta_two) * gradient * gradient
    update = new_first / bias_one / (jnp.sqrt(new_second / bias_two) + adam_epsilon)
    new_master = master_rows - learn_rate * (update + decay_rate * master_rows)
    new_teacher = ema_momentum * teacher_rows + (1.0 - ema_momentum) * new_master
    return (new_master, new_first, new_second, new_teacher)


def swap(block):
    return lax.ppermute(block, "core", SWAP)


def in_order(mine, theirs, axis_name, axis):
    first = lax.axis_index(axis_name) == 0
    return jnp.where(
        first,
        jnp.concatenate([mine, theirs], axis=axis),
        jnp.concatenate([theirs, mine], axis=axis),
    )


def columns_of(array, core):
    half = array.shape[-1] // 2
    return lax.dynamic_slice_in_dim(array, core * half, half, axis=array.ndim - 1)


def half_block(rows, core):
    return in_order(columns_of(rows, core), swap(columns_of(rows, 1 - core)), "core", 0)


def copies_of(block):
    return jnp.broadcast_to(block[None], (32,) + block.shape)


def exchanged(blocks, chips=CHIPS):
    return lax.all_to_all(blocks, chips, 0, 0, tiled=True)


def copies_kernel(block_ref, copies_ref):
    copies_ref[...] = jnp.broadcast_to(block_ref[...][None], copies_ref.shape)


def copies_call(block, count, steps):
    return pl.pallas_call(
        copies_kernel,
        grid=(steps,),
        in_specs=[pl.BlockSpec(block.shape, lambda i: (0, 0))],
        out_specs=pl.BlockSpec((count // steps,) + block.shape, lambda i: (i, 0, 0)),
        out_shape=jax.ShapeDtypeStruct((count,) + block.shape, block.dtype),
        compiler_params=params(LIMIT),
        cost_estimate=cost(0, 1024),
    )(block)


def norm_kernel(tokens_ref, normed_ref):
    normed_ref[...] = layer_norm(tokens_ref[...])[0].astype(bf16)


def norm_call(tokens, steps):
    rows, width = tokens.shape
    spec = pl.BlockSpec((rows // steps, width), lambda i: (i, 0))
    return pl.pallas_call(
        norm_kernel,
        grid=(steps,),
        in_specs=[spec],
        out_specs=spec,
        out_shape=jax.ShapeDtypeStruct(tokens.shape, bf16),
        compiler_params=params(LIMIT),
        cost_estimate=cost(0, 1024),
    )(tokens)


LIMIT = 62
TILES = ((0, 512), (512, 512), (1024, 544))
PIECES = 4


def start_all(copies):
    for copy in copies:
        copy.start()
    return copies


def wait_all(copies):
    for copy in copies:
        copy.wait()


def store_delta(which_ref, hbm, vmem, sems):
    normed_hbm, weights_hbm, cotangent_hbm, delta_hbm = hbm
    normed_ref, weights_ref, cotangent_ref, delta_ref = vmem
    half = weights_ref.shape[1]
    columns = pl.ds(pl.multiple_of(which_ref[0] * half, half), half)
    weights_in = start_all([pltpu.make_async_copy(weights_hbm, weights_ref, sems.at[0])])
    tiles_in = []
    for n, (first, size) in enumerate(TILES):
        rows = pl.ds(first, size)
        tiles_in.append(
            start_all(
                [
                    pltpu.make_async_copy(
                        normed_hbm.at[rows], normed_ref.at[rows], sems.at[1 + 2 * n]
                    ),
                    pltpu.make_async_copy(
                        cotangent_hbm.at[rows, columns], cotangent_ref.at[rows], sems.at[2 + 2 * n]
                    ),
                ]
            )
        )
    out = []
    wait_all(weights_in)
    for n, (first, size) in enumerate(TILES):
        rows = pl.ds(first, size)
        wait_all(tiles_in[n])
        for m in range(0, half, 256):
            part = pl.ds(m, 256)
            preact = jnp.dot(normed_ref[rows, :], weights_ref[:, part], preferred_element_type=f32)
            slope = gelu_parts(preact)[1]
            delta_ref[rows, part] = (cotangent_ref[rows, part].astype(f32) * slope).astype(bf16)
        copy = pltpu.make_async_copy(delta_ref.at[rows], delta_hbm.at[rows], sems.at[7 + n])
        out += start_all([copy])
    return out


def gradient_piece(normed_ref, delta_ref, n, step):
    return lax.dot_general(
        normed_ref[:, n * step : (n + 1) * step],
        delta_ref[...],
        (((0,), (0,)), ((), ())),
        preferred_element_type=f32,
    )


def own_kernel(which_ref, normed_hbm, weights_hbm, cotangent_hbm, delta_hbm, *refs):
    sums_hbm, vmem, (sums_ref, sems) = refs[:PIECES], refs[PIECES:-2], refs[-2:]
    hbm = (normed_hbm, weights_hbm, cotangent_hbm, delta_hbm)
    out = store_delta(which_ref, hbm, vmem, sems)
    step = sums_ref.shape[0] // PIECES
    for n in range(PIECES):
        rows = pl.ds(n * step, step)
        sums_ref[rows, :] = gradient_piece(vmem[0], vmem[3], n, step).astype(bf16)
        copy = pltpu.make_async_copy(sums_ref.at[rows], sums_hbm[n], sems.at[10 + n])
        out += start_all([copy])
    wait_all(out)


def other_kernel(which_ref, normed_hbm, weights_hbm, cotangent_hbm, delta_hbm, *refs):
    hbm = (normed_hbm, weights_hbm, cotangent_hbm, delta_hbm)
    wait_all(store_delta(which_ref, hbm, refs[:-1], refs[-1]))


def sum_kernel(normed_hbm, delta_hbm, *refs):
    got_hbm, (sums_hbm, normed_ref, delta_ref, got_ref, sums_ref, sems) = refs[:PIECES], refs[PIECES:]
    step = sums_ref.shape[0] // PIECES
    delta_in = start_all([pltpu.make_async_copy(delta_hbm, delta_ref, sems.at[0])])
    pieces_in = []
    for n in range(PIECES):
        columns, rows = pl.ds(n * step, step), pl.ds(n * step, step)
        pieces_in.append(
            start_all(
                [
                    pltpu.make_async_copy(
                        normed_hbm.at[:, columns], normed_ref.at[:, columns], sems.at[1 + 2 * n]
                    ),
                    pltpu.make_async_copy(got_hbm[n], got_ref.at[rows], sems.at[2 + 2 * n]),
                ]
            )
        )
    out = []
    wait_all(delta_in)
    for n in range(PIECES):
        rows = pl.ds(n * step, step)
        wait_all(pieces_in[n])
        total = gradient_piece(normed_ref, delta_ref, n, step) + got_ref[rows, :].astype(f32)
        sums_ref[rows, :] = total.astype(bf16)
        copy = pltpu.make_async_copy(
            sums_ref.at[rows], sums_hbm.at[rows], sems.at[1 + 2 * PIECES + n]
        )
        out += start_all([copy])
    wait_all(out)


def local_call(kernel, outs, scratch, semaphores, *arrays):
    anywhere = pl.BlockSpec(memory_space=pl.ANY)
    return pl.pallas_call(
        kernel,
        in_specs=[
            pl.BlockSpec(memory_space=pltpu.SMEM) if array.ndim == 1 else anywhere
            for array in arrays
        ],
        out_specs=[anywhere] * len(outs),
        out_shape=[jax.ShapeDtypeStruct(shape, bf16) for shape in outs],
        scratch_shapes=[pltpu.VMEM(shape, bf16) for shape in scratch]
        + [pltpu.SemaphoreType.DMA((semaphores,))],
        compiler_params=params(LIMIT),
        cost_estimate=cost(0, 1024),
    )(*arrays)


def input_kernel(delta_own_ref, delta_other_ref, own_ref, other_ref, tokens_ref, out_ref):
    dims = (((1,), (1,)), ((), ()))
    back = lax.dot_general(delta_own_ref[...], own_ref[...], dims, preferred_element_type=f32)
    back += lax.dot_general(delta_other_ref[...], other_ref[...], dims, preferred_element_type=f32)
    centred, inv_std = layer_norm(tokens_ref[...])
    mean_back = jnp.mean(back, axis=-1, keepdims=True)
    mean_cross = jnp.mean(back * centred, axis=-1, keepdims=True)
    out_ref[...] = (inv_std * (back - mean_back - centred * mean_cross)).astype(bf16)


def input_call(delta_own, delta_other, own, other, tokens):
    rows, width = tokens.shape
    half = own.shape[1]
    deltas = pl.BlockSpec((784, half), lambda i: (i, 0))
    weights = pl.BlockSpec((width, half), lambda i: (0, 0))
    spec = pl.BlockSpec((784, width), lambda i: (i, 0))
    return pl.pallas_call(
        input_kernel,
        grid=(rows // 784,),
        in_specs=[deltas, deltas, weights, weights, spec],
        out_specs=spec,
        out_shape=jax.ShapeDtypeStruct((rows, width), bf16),
        compiler_params=params(60),
        cost_estimate=cost(4 * rows * width * half, 0),
    )(delta_own, delta_other, own, other, tokens)


def hidden_kernel(core_ref, normed_ref, own_ref, other_ref, hidden_ref):
    normed = normed_ref[...]
    half, step = own_ref.shape[1], 256
    for which, weights_ref in ((0, own_ref), (1, other_ref)):
        start = jnp.where(core_ref[0] == which, 0, half)
        for n in range(0, half, step):
            pre = jnp.dot(normed, weights_ref[:, n : n + step], preferred_element_type=f32)
            columns = pl.ds(pl.multiple_of(start + n, step), step)
            hidden_ref[:, columns] = gelu_parts(pre)[0].astype(bf16)


def hidden_call(normed, own, other, core):
    rows, width = normed.shape
    half, tile = own.shape[1], rows
    weights = pl.BlockSpec((width, half), lambda i, core: (0, 0))
    return pl.pallas_call(
        hidden_kernel,
        grid_spec=pltpu.PrefetchScalarGridSpec(
            num_scalar_prefetch=1,
            grid=(rows // tile,),
            in_specs=[pl.BlockSpec((tile, width), lambda i, core: (i, 0)), weights, weights],
            out_specs=pl.BlockSpec((tile, 2 * half), lambda i, core: (i, 0)),
        ),
        out_shape=jax.ShapeDtypeStruct((rows, 2 * half), bf16),
        compiler_params=params(60),
        cost_estimate=cost(4 * rows * width * half, 0),
    )(core.astype(jnp.int32).reshape(1), normed, own, other)


def per_device(tokens, cotangent, global_tokens, master, first_moment, second_moment, teacher):
    core = lax.axis_index("core")

    width, half = tokens.shape[1], cotangent.shape[1] // 2

    copies = copies_of(half_block(master.astype(bf16), core))
    copies, tokens, global_tokens, teacher_rows = lax.optimization_barrier(
        (copies, tokens, global_tokens, teacher)
    )
    weights_own = exchanged(copies).reshape(width, half)
    teacher_block = half_block(teacher_rows.astype(bf16), core)
    beyond = lax.ppermute(teacher_block, ("yh", "yl"), ACROSS)
    teacher_block = in_order(teacher_block, beyond, "yh", 0)
    teacher_copies = copies_call(teacher_block, 16, 1)
    normed, teacher_normed = norm_call(tokens, 2), norm_call(global_tokens, 1)
    normed, teacher_normed, teacher_copies, weights_own = lax.optimization_barrier(
        (normed, teacher_normed, teacher_copies, weights_own)
    )
    teacher_own = exchanged(teacher_copies, ("z", "x")).reshape(width, half)
    weights_other = swap(weights_own)

    rows = tokens.shape[0]
    delta, square = (rows, half), (width, half)
    vmem = [(rows, width), square, delta, delta]
    which = core.astype(jnp.int32).reshape(1)
    delta_own, *given = local_call(
        own_kernel,
        [delta] + [(width // PIECES, half)] * PIECES,
        vmem + [square],
        10 + PIECES,
        which,
        normed,
        weights_own,
        cotangent,
    )
    got = [swap(piece) for piece in given]
    (delta_other,) = local_call(
        other_kernel, [delta], vmem, 10, 1 - which, normed, weights_other, cotangent
    )
    (partial,) = local_call(
        sum_kernel,
        [square],
        [(rows, width), delta, square, square],
        1 + 3 * PIECES,
        normed,
        delta_other,
        *got,
    )
    pieces = exchanged(partial.reshape(32, 32, half))
    partial, delta_own, delta_other, teacher_own = lax.optimization_barrier(
        (partial, delta_own, delta_other, teacher_own)
    )
    grad_input = input_call(delta_own, delta_other, weights_own, weights_other, tokens)
    teacher_hidden = hidden_call(teacher_normed, teacher_own, swap(teacher_own), core)
    pieces, teacher_hidden, grad_input = lax.optimization_barrier(
        (pieces, teacher_hidden, grad_input)
    )
    group = jnp.sum(pieces.astype(f32), axis=0)
    group = lax.optimization_barrier(group.astype(bf16))
    mine = lax.dynamic_slice_in_dim(group, core * 16, 16, axis=0)
    other = lax.dynamic_slice_in_dim(group, (1 - core) * 16, 16, axis=0)
    here = mine.astype(f32) + lax.ppermute(mine, "yl", SWAP).astype(f32)
    diagonal = lax.ppermute(other, ("core", "yl"), [(0, 3), (1, 2), (2, 1), (3, 0)])
    there = swap(other).astype(f32) + diagonal.astype(f32)
    gradient = in_order(there, here, "core", 1)
    new_master, new_first, new_second, new_teacher = adamw_update(
        gradient, master, first_moment, second_moment, teacher
    )
    return (grad_input, teacher_hidden, new_master, new_first, new_second, new_teacher)


def solution(mesh):
    names = ("z", "x", "yh", "core", "yl")
    split = Mesh(mesh.devices.reshape(4, 4, 2, 2, 2), names)
    tokens = P(names, None)
    rows = P(names[:-1], None)
    return jax.shard_map(
        per_device,
        mesh=split,
        in_specs=(tokens, tokens, tokens, rows, rows, rows, rows),
        out_specs=(tokens, tokens, rows, rows, rows, rows),
        check_vma=False,
    )
```

```python
import math

import jax
import jax.numpy as jnp
from jax import lax
from jax.experimental import pallas as pl
from jax.experimental.pallas import tpu as pltpu
from jax.sharding import Mesh
from jax.sharding import PartitionSpec as P

beta_one = 0.9
beta_two = 0.999
learn_rate = 0.001
decay_rate = 0.04
ema_momentum = 0.996
adam_epsilon = 1e-08
norm_epsilon = 1e-06
bias_one = 0.9999734386011124
bias_two = 0.09520785288629038

SWAP = [(0, 1), (1, 0)]
ACROSS = [(0, 3), (3, 0), (1, 2), (2, 1)]
CHIPS = ("z", "x", "yh")
bf16, f32 = jnp.bfloat16, jnp.float32


def params(mebibytes):
    return pltpu.CompilerParams(vmem_limit_bytes=mebibytes * 1024 * 1024)


def cost(flops, bytes_accessed):
    return pl.CostEstimate(flops=flops, bytes_accessed=bytes_accessed, transcendentals=0)


def layer_norm(block_tokens):
    values = block_tokens.astype(f32)
    middle = jnp.mean(values, axis=-1, keepdims=True)
    centred = values - middle
    inv_std = lax.rsqrt(jnp.mean(centred * centred, axis=-1, keepdims=True) + norm_epsilon)
    return (centred * inv_std, inv_std)


def gelu_parts(preact):
    cumul = 0.5 * (1.0 + lax.erf(preact * (1.0 / math.sqrt(2.0))))
    slope = cumul + preact * jnp.exp(-0.5 * preact * preact) * (1.0 / math.sqrt(2.0 * math.pi))
    return (preact * cumul, slope)


def adamw_update(gradient, master_rows, first_rows, second_rows, teacher_rows):
    new_first = beta_one * first_rows + (1.0 - beta_one) * gradient
    new_second = beta_two * second_rows + (1.0 - beta_two) * gradient * gradient
    update = new_first / bias_one / (jnp.sqrt(new_second / bias_two) + adam_epsilon)
    new_master = master_rows - learn_rate * (update + decay_rate * master_rows)
    new_teacher = ema_momentum * teacher_rows + (1.0 - ema_momentum) * new_master
    return (new_master, new_first, new_second, new_teacher)


def swap(block):
    return lax.ppermute(block, "core", SWAP)


def in_order(mine, theirs, axis_name, axis):
    first = lax.axis_index(axis_name) == 0
    return jnp.where(
        first,
        jnp.concatenate([mine, theirs], axis=axis),
        jnp.concatenate([theirs, mine], axis=axis),
    )


def columns_of(array, core):
    half = array.shape[-1] // 2
    return lax.dynamic_slice_in_dim(array, core * half, half, axis=array.ndim - 1)


def half_block(rows, core):
    return in_order(columns_of(rows, core), swap(columns_of(rows, 1 - core)), "core", 0)


def copies_of(block):
    return jnp.broadcast_to(block[None], (32,) + block.shape)


def exchanged(blocks, chips=CHIPS):
    return lax.all_to_all(blocks, chips, 0, 0, tiled=True)


def copies_kernel(place_ref, block_ref, beyond_ref, copies_hbm, whole_ref, sems):
    first, size = place_ref[0] == 0, block_ref.shape[0]
    mine, theirs = block_ref[...], beyond_ref[...]
    whole_ref[:size, :] = jnp.where(first, mine, theirs)
    whole_ref[size:, :] = jnp.where(first, theirs, mine)
    out = [
        pltpu.make_async_copy(whole_ref, copies_hbm.at[n], sems.at[n])
        for n in range(copies_hbm.shape[0])
    ]
    for copy in out:
        copy.start()
    for copy in out:
        copy.wait()


def copies_call(place, block, beyond):
    shape = (2 * block.shape[0], block.shape[1])
    return pl.pallas_call(
        copies_kernel,
        in_specs=[
            pl.BlockSpec(memory_space=pltpu.SMEM),
            pl.BlockSpec(memory_space=pltpu.VMEM),
            pl.BlockSpec(memory_space=pltpu.VMEM),
        ],
        out_specs=pl.BlockSpec(memory_space=pl.ANY),
        out_shape=jax.ShapeDtypeStruct((16,) + shape, block.dtype),
        scratch_shapes=[pltpu.VMEM(shape, block.dtype), pltpu.SemaphoreType.DMA((16,))],
        compiler_params=params(LIMIT),
        cost_estimate=cost(0, 1024),
    )(place.astype(jnp.int32).reshape(1), block, beyond)


def norm_kernel(tokens_ref, normed_ref):
    normed_ref[...] = layer_norm(tokens_ref[...])[0].astype(bf16)


def norm_call(tokens, steps):
    rows, width = tokens.shape
    spec = pl.BlockSpec((rows // steps, width), lambda i: (i, 0))
    return pl.pallas_call(
        norm_kernel,
        grid=(steps,),
        in_specs=[spec],
        out_specs=spec,
        out_shape=jax.ShapeDtypeStruct(tokens.shape, bf16),
        compiler_params=params(LIMIT),
        cost_estimate=cost(0, 1024),
    )(tokens)


LIMIT = 62
TILES = ((0, 512), (512, 512), (1024, 544))
PIECES = 2


def start_all(copies):
    for copy in copies:
        copy.start()
    return copies


def wait_all(copies):
    for copy in copies:
        copy.wait()


def store_delta(which_ref, hbm, vmem, sems):
    normed_hbm, weights_hbm, cotangent_hbm, delta_hbm = hbm
    normed_ref, weights_ref, cotangent_ref, delta_ref = vmem
    half = weights_ref.shape[1]
    columns = pl.ds(pl.multiple_of(which_ref[0] * half, half), half)
    weights_in = start_all([pltpu.make_async_copy(weights_hbm, weights_ref, sems.at[0])])
    tiles_in = []
    for n, (first, size) in enumerate(TILES):
        rows = pl.ds(first, size)
        tiles_in.append(
            start_all(
                [
                    pltpu.make_async_copy(
                        normed_hbm.at[rows], normed_ref.at[rows], sems.at[1 + 2 * n]
                    ),
                    pltpu.make_async_copy(
                        cotangent_hbm.at[rows, columns], cotangent_ref.at[rows], sems.at[2 + 2 * n]
                    ),
                ]
            )
        )
    out = []
    wait_all(weights_in)
    for n, (first, size) in enumerate(TILES):
        rows = pl.ds(first, size)
        wait_all(tiles_in[n])
        for m in range(0, half, 256):
            part = pl.ds(m, 256)
            preact = jnp.dot(normed_ref[rows, :], weights_ref[:, part], preferred_element_type=f32)
            slope = gelu_parts(preact)[1]
            delta_ref[rows, part] = (cotangent_ref[rows, part].astype(f32) * slope).astype(bf16)
        copy = pltpu.make_async_copy(delta_ref.at[rows], delta_hbm.at[rows], sems.at[7 + n])
        out += start_all([copy])
    return out


def gradient_piece(normed_ref, delta_ref, n, step):
    return lax.dot_general(
        normed_ref[:, n * step : (n + 1) * step],
        delta_ref[...],
        (((0,), (0,)), ((), ())),
        preferred_element_type=f32,
    )


def own_kernel(which_ref, normed_hbm, weights_hbm, cotangent_hbm, delta_hbm, *refs):
    sums_hbm, vmem, (sums_ref, sems) = refs[:PIECES], refs[PIECES:-2], refs[-2:]
    hbm = (normed_hbm, weights_hbm, cotangent_hbm, delta_hbm)
    out = store_delta(which_ref, hbm, vmem, sems)
    step = sums_ref.shape[0] // PIECES
    for n in range(PIECES):
        rows = pl.ds(n * step, step)
        sums_ref[rows, :] = gradient_piece(vmem[0], vmem[3], n, step).astype(bf16)
        copy = pltpu.make_async_copy(sums_ref.at[rows], sums_hbm[n], sems.at[10 + n])
        out += start_all([copy])
    wait_all(out)


def other_kernel(which_ref, normed_hbm, weights_hbm, cotangent_hbm, delta_hbm, *refs):
    hbm = (normed_hbm, weights_hbm, cotangent_hbm, delta_hbm)
    wait_all(store_delta(which_ref, hbm, refs[:-1], refs[-1]))


def sum_kernel(normed_hbm, delta_hbm, *refs):
    got_hbm, (sums_hbm, normed_ref, delta_ref, got_ref, sums_ref, sems) = refs[:PIECES], refs[PIECES:]
    step = sums_ref.shape[0] // PIECES
    delta_in = start_all([pltpu.make_async_copy(delta_hbm, delta_ref, sems.at[0])])
    pieces_in = []
    for n in range(PIECES):
        columns, rows = pl.ds(n * step, step), pl.ds(n * step, step)
        pieces_in.append(
            start_all(
                [
                    pltpu.make_async_copy(
                        normed_hbm.at[:, columns], normed_ref.at[:, columns], sems.at[1 + 2 * n]
                    ),
                    pltpu.make_async_copy(got_hbm[n], got_ref.at[rows], sems.at[2 + 2 * n]),
                ]
            )
        )
    out = []
    wait_all(delta_in)
    for n in range(PIECES):
        rows = pl.ds(n * step, step)
        wait_all(pieces_in[n])
        total = gradient_piece(normed_ref, delta_ref, n, step) + got_ref[rows, :].astype(f32)
        sums_ref[rows, :] = total.astype(bf16)
        copy = pltpu.make_async_copy(
            sums_ref.at[rows], sums_hbm.at[rows], sems.at[1 + 2 * PIECES + n]
        )
        out += start_all([copy])
    wait_all(out)


def local_call(kernel, outs, scratch, semaphores, *arrays):
    anywhere = pl.BlockSpec(memory_space=pl.ANY)
    return pl.pallas_call(
        kernel,
        in_specs=[
            pl.BlockSpec(memory_space=pltpu.SMEM) if array.ndim == 1 else anywhere
            for array in arrays
        ],
        out_specs=[anywhere] * len(outs),
        out_shape=[jax.ShapeDtypeStruct(shape, bf16) for shape in outs],
        scratch_shapes=[pltpu.VMEM(shape, bf16) for shape in scratch]
        + [pltpu.SemaphoreType.DMA((semaphores,))],
        compiler_params=params(LIMIT),
        cost_estimate=cost(0, 1024),
    )(*arrays)


def input_kernel(delta_own_ref, delta_other_ref, own_ref, other_ref, tokens_ref, out_ref):
    dims = (((1,), (1,)), ((), ()))
    back = lax.dot_general(delta_own_ref[...], own_ref[...], dims, preferred_element_type=f32)
    back += lax.dot_general(delta_other_ref[...], other_ref[...], dims, preferred_element_type=f32)
    centred, inv_std = layer_norm(tokens_ref[...])
    mean_back = jnp.mean(back, axis=-1, keepdims=True)
    mean_cross = jnp.mean(back * centred, axis=-1, keepdims=True)
    out_ref[...] = (inv_std * (back - mean_back - centred * mean_cross)).astype(bf16)


def input_call(delta_own, delta_other, own, other, tokens):
    rows, width = tokens.shape
    half = own.shape[1]
    deltas = pl.BlockSpec((784, half), lambda i: (i, 0))
    weights = pl.BlockSpec((width, half), lambda i: (0, 0))
    spec = pl.BlockSpec((784, width), lambda i: (i, 0))
    return pl.pallas_call(
        input_kernel,
        grid=(rows // 784,),
        in_specs=[deltas, deltas, weights, weights, spec],
        out_specs=spec,
        out_shape=jax.ShapeDtypeStruct((rows, width), bf16),
        compiler_params=params(60),
        cost_estimate=cost(4 * rows * width * half, 0),
    )(delta_own, delta_other, own, other, tokens)


def hidden_kernel(core_ref, normed_ref, own_ref, other_ref, hidden_ref):
    normed = normed_ref[...]
    half, step = own_ref.shape[1], 256
    for which, weights_ref in ((0, own_ref), (1, other_ref)):
        start = jnp.where(core_ref[0] == which, 0, half)
        for n in range(0, half, step):
            pre = jnp.dot(normed, weights_ref[:, n : n + step], preferred_element_type=f32)
            columns = pl.ds(pl.multiple_of(start + n, step), step)
            hidden_ref[:, columns] = gelu_parts(pre)[0].astype(bf16)


def hidden_call(normed, own, other, core):
    rows, width = normed.shape
    half, tile = own.shape[1], rows
    weights = pl.BlockSpec((width, half), lambda i, core: (0, 0))
    return pl.pallas_call(
        hidden_kernel,
        grid_spec=pltpu.PrefetchScalarGridSpec(
            num_scalar_prefetch=1,
            grid=(rows // tile,),
            in_specs=[pl.BlockSpec((tile, width), lambda i, core: (i, 0)), weights, weights],
            out_specs=pl.BlockSpec((tile, 2 * half), lambda i, core: (i, 0)),
        ),
        out_shape=jax.ShapeDtypeStruct((rows, 2 * half), bf16),
        compiler_params=params(60),
        cost_estimate=cost(4 * rows * width * half, 0),
    )(core.astype(jnp.int32).reshape(1), normed, own, other)


def per_device(tokens, cotangent, global_tokens, master, first_moment, second_moment, teacher):
    core = lax.axis_index("core")

    width, half = tokens.shape[1], cotangent.shape[1] // 2

    copies = copies_of(half_block(master.astype(bf16), core))
    copies, tokens, global_tokens, teacher_rows = lax.optimization_barrier(
        (copies, tokens, global_tokens, teacher)
    )
    weights_own = exchanged(copies).reshape(width, half)
    teacher_block = half_block(teacher_rows.astype(bf16), core)
    beyond = lax.ppermute(teacher_block, ("yh", "yl"), ACROSS)
    teacher_copies = copies_call(lax.axis_index("yh"), teacher_block, beyond)
    normed, teacher_normed = norm_call(tokens, 2), norm_call(global_tokens, 1)
    normed, teacher_normed, teacher_copies, weights_own = lax.optimization_barrier(
        (normed, teacher_normed, teacher_copies, weights_own)
    )
    teacher_own = exchanged(teacher_copies, ("z", "x")).reshape(width, half)
    weights_other = swap(weights_own)

    rows = tokens.shape[0]
    delta, square = (rows, half), (width, half)
    vmem = [(rows, width), square, delta, delta]
    which = core.astype(jnp.int32).reshape(1)
    delta_own, *given = local_call(
        own_kernel,
        [delta] + [(width // PIECES, half)] * PIECES,
        vmem + [square],
        10 + PIECES,
        which,
        normed,
        weights_own,
        cotangent,
    )
    got = [swap(piece) for piece in given]
    (delta_other,) = local_call(
        other_kernel, [delta], vmem, 10, 1 - which, normed, weights_other, cotangent
    )
    (partial,) = local_call(
        sum_kernel,
        [square],
        [(rows, width), delta, square, square],
        1 + 3 * PIECES,
        normed,
        delta_other,
        *got,
    )
    pieces = exchanged(partial.reshape(32, 32, half))
    partial, delta_own, delta_other, teacher_own = lax.optimization_barrier(
        (partial, delta_own, delta_other, teacher_own)
    )
    grad_input = input_call(delta_own, delta_other, weights_own, weights_other, tokens)
    teacher_hidden = hidden_call(teacher_normed, teacher_own, swap(teacher_own), core)
    pieces, teacher_hidden, grad_input = lax.optimization_barrier(
        (pieces, teacher_hidden, grad_input)
    )
    group = jnp.sum(pieces.astype(f32), axis=0)
    group = lax.optimization_barrier(group.astype(bf16))
    mine = lax.dynamic_slice_in_dim(group, core * 16, 16, axis=0)
    other = lax.dynamic_slice_in_dim(group, (1 - core) * 16, 16, axis=0)
    here = mine.astype(f32) + lax.ppermute(mine, "yl", SWAP).astype(f32)
    diagonal = lax.ppermute(other, ("core", "yl"), [(0, 3), (1, 2), (2, 1), (3, 0)])
    there = swap(other).astype(f32) + diagonal.astype(f32)
    gradient = in_order(there, here, "core", 1)
    new_master, new_first, new_second, new_teacher = adamw_update(
        gradient, master, first_moment, second_moment, teacher
    )
    return (grad_input, teacher_hidden, new_master, new_first, new_second, new_teacher)


def solution(mesh):
    names = ("z", "x", "yh", "core", "yl")
    split = Mesh(mesh.devices.reshape(4, 4, 2, 2, 2), names)
    tokens = P(names, None)
    rows = P(names[:-1], None)
    return jax.shard_map(
        per_device,
        mesh=split,
        in_specs=(tokens, tokens, tokens, rows, rows, rows, rows),
        out_specs=(tokens, tokens, rows, rows, rows, rows),
        check_vma=False,
    )
```
